32 devices in a mesh: group: 2 (over y), wide: 4 (over z), narrow: 2 (over x), deep: 2 (over core).
Axes of the slice: x: 2, y: 2, z: 4, core: 2. Of those that a mesh axis runs over, the one named last changes fastest.
Arguments:
- queries: bfloat16 [384, 4096], P(('group', 'wide', 'deep'), 'narrow'), parts along dimension 0, may hold values from -110 to 110
- cache_keys: bfloat16 [384, 4, 32, 128], P(('group', 'wide', 'deep'), 'narrow'), parts along dimension 0, may hold values from -4.1 to 4.1
- cache_values: bfloat16 [384, 4, 32, 128], P(('group', 'wide', 'deep'), 'narrow'), parts along dimension 0, may hold values from -6 to 6
- fresh_pairs: bfloat16 [384, 2, 512], P(('group', 'wide', 'deep'), None, 'narrow'), parts along dimension 0, may hold values from -6 to 6
- lengths: int32 [384], P(('group', 'wide', 'deep')), parts along dimension 0, may hold values from 2 to 32, as said below
- residual: bfloat16 [384, 2048], P(('group', 'wide', 'deep')), parts along dimension 0, may hold values from -6 to 6
- norm_gain: float32 [2048], replicated, may hold values from 0.1 to 1.9
- output_weight: bfloat16 [4096, 2048], P('narrow', 'deep'), may hold values from -0.09375 to 0.09375
- expert_gate_up: bfloat16 [8, 2, 768, 2048], P(('wide', 'deep'), None, 'narrow'), may hold values from -0.125 to 0.125
- expert_down: bfloat16 [8, 768, 2048], P(('wide', 'deep'), None, 'narrow'), may hold values from -0.21875 to 0.21875
- routed_experts: int32 [384, 1], P(('group', 'wide', 'deep')), parts along dimension 0, may hold values from 0 to 7, as said below
- router_weights: float32 [384, 1], P(('group', 'wide', 'deep')), parts along dimension 0, may hold values from 0.1 to 1
Outputs:
- layer_out: bfloat16 [384, 2048], P(('group', 'wide', 'deep'), 'narrow'), parts along dimension 0
The draws below stay inside these ranges and needn't reach their ends.
There are 2 independent parts, one for each index of `group`. The reference program is written for one: setup_inputs(seed, part) draws one part's arguments, and reference() takes and returns one part's arrays. A program takes and returns all parts, laid end to end along the dimension named above; an argument that names none is the same for every part. Nothing has to cross between parts.
Inputs may be any that keep to these rules, and one draw needn't show every extreme that they name: `routed_experts`: each row names 1 different experts. Among the rows of one device no expert is named more than 6 times, and one and the same expert is named exactly 6 times by the rows of every device. `lengths`: each device's block of 24 requests holds one of length 32.
All inputs are finite; a program needn't handle non-finite values.
Results may differ from the reference program's by a relative error of at most 0.0095.
Values may be sent and summed in bfloat16 or wider, within the bound.
A program may use at most 64 MiB of HBM per device.

```python
import math
import jax
import jax.numpy as jnp
from jax import lax

D = 2048
QH = 32
KVH = 4
HD = 128
FFE = 768
REQ_DEV = 24
CACHE_LEN = 32
EXPERTS = 8
TOPK = 1
TOKENS = 192


def key_field(key):
    field = jnp.clip(jax.random.normal(jax.random.fold_in(key, 101), (TOKENS, KVH, CACHE_LEN, HD), jnp.float32), -4.0, 4.0)
    return field


def draw_cache_keys(key, part):
    return key_field(key).astype(jnp.bfloat16)


def draw_queries(key, part):
    base_draw = jnp.clip(jax.random.normal(jax.random.fold_in(key, 202), (TOKENS, QH, HD), jnp.float32), -5.0, 5.0)
    return base_draw.reshape(TOKENS, QH * HD).astype(jnp.bfloat16)


def draw_lengths(key, part):
    block_count = TOKENS // REQ_DEV
    base_draw = jax.random.randint(jax.random.fold_in(key, 303), (block_count, REQ_DEV), 2, CACHE_LEN + 1)
    full_place = jax.random.randint(jax.random.fold_in(key, 304), (block_count, 1), 0, REQ_DEV)
    base_draw = jnp.where(jnp.arange(REQ_DEV)[None, :] == full_place, CACHE_LEN, base_draw)
    return base_draw.reshape(TOKENS).astype(jnp.int32)


def draw_routed_experts(key, part):
    block_count = TOKENS // REQ_DEV
    capacity = REQ_DEV // 4
    hottest = jax.random.randint(jax.random.fold_in(key, 401), (), 0, EXPERTS)

    def one_block(subkey):
        first_key, second_key, third_key = jax.random.split(subkey, 3)
        ranking = jax.random.permutation(first_key, EXPERTS) + 1
        ranking = jnp.where(jnp.arange(EXPERTS) == hottest, 0, ranking)
        ordering = jnp.argsort(ranking)
        segments = jax.random.randint(second_key, (), 5, 9)
        request_rank = jnp.arange(REQ_DEV)
        segment_of = jnp.where(request_rank < capacity, 0, 1 + (request_rank - capacity) % (segments - 1))
        segment_of = jax.random.permutation(third_key, segment_of)
        return ordering[segment_of[:, None] * TOPK + jnp.arange(TOPK)[None, :]]
    block_keys = jax.random.split(jax.random.fold_in(key, 402), block_count)
    return jax.vmap(one_block)(block_keys).reshape(TOKENS, TOPK).astype(jnp.int32)


def level_of(key, extent, cuts, low, largest):
    level = 1.0
    for axis_at, shards_of in cuts:
        steps = jax.random.uniform(jax.random.fold_in(jax.random.fold_in(key, 6), axis_at), (shards_of,), jnp.float32, low / len(cuts), largest / len(cuts))
        level = level * jnp.repeat(jnp.exp(steps), extent[axis_at] // shards_of).reshape((-1,) + (1,) * (len(extent) - 1 - axis_at))
    return level


def bell_draw(rng, extent, width, bound, pieces=(), kind=jnp.bfloat16):
    drawn = jax.random.normal(rng, extent, jnp.float32) * width
    if len(pieces) > 0:
        drawn = level_of(rng, extent, pieces, -0.22, 0.18) * drawn
    return jnp.clip(drawn, min=-bound, max=bound).astype(kind)


def setup_inputs(seed: int = 0, part: int = 0) -> dict:
    splits = jax.random.split(jax.random.key(seed), 13)
    part_splits = jax.random.split(jax.random.fold_in(splits[12], part), 13)
    return {
        "queries": draw_queries(jax.random.fold_in(jax.random.fold_in(splits[12], part), 71), part),
        "cache_keys": draw_cache_keys(jax.random.fold_in(jax.random.fold_in(splits[12], part), 71), part),
        "cache_values": bell_draw(part_splits[2], (TOKENS, KVH, CACHE_LEN, HD), 1.0, 6.0, ((0, 8), (1, 2))),
        "fresh_pairs": bell_draw(part_splits[3], (TOKENS, 2, KVH * HD), 1.0, 6.0, ((0, 8), (2, 2))),
        "lengths": draw_lengths(jax.random.fold_in(jax.random.fold_in(splits[12], part), 71), part),
        "residual": bell_draw(part_splits[5], (TOKENS, D), 1.0, 6.0, ((0, 8),)),
        "norm_gain": jnp.clip(1.0 + 0.18 * jax.random.normal(splits[6], (D,), jnp.float32), 0.1, 1.9),
        "output_weight": bell_draw(splits[7], (QH * HD, D), (QH * HD) ** -0.5, 0.09375, ((0, 2), (1, 2))),
        "expert_gate_up": bell_draw(splits[8], (EXPERTS, 2, FFE, D), D ** -0.5, 0.125, ((0, 8), (2, 2))),
        "expert_down": bell_draw(splits[9], (EXPERTS, FFE, D), FFE ** -0.5, 0.21875, ((0, 8), (2, 2))),
        "routed_experts": draw_routed_experts(jax.random.fold_in(jax.random.fold_in(splits[12], part), 71), part),
        "router_weights": jnp.clip(jnp.exp(math.log(1.0) - 2.3025851 * jax.random.uniform(part_splits[11], (TOKENS, TOPK), jnp.float32) ** level_of(part_splits[11], (TOKENS, TOPK), ((0, 8),), -0.2, 0.2)), 0.1, 1.0),
    }


def reference(queries, cache_keys, cache_values, fresh_pairs, lengths, residual, norm_gain, output_weight, expert_gate_up, expert_down, routed_experts, router_weights):
    group_size = QH // KVH
    score_scale = 1.0 / math.sqrt(HD)
    query_heads = queries.astype(jnp.float32).reshape(TOKENS, KVH, group_size, HD)
    keys_float = cache_keys.astype(jnp.float32)
    values_float = cache_values.astype(jnp.float32)
    fresh_heads = fresh_pairs.astype(jnp.float32).reshape(TOKENS, 2, KVH, HD)
    scores = jnp.einsum('tkgd,tkld->tkgl', query_heads, keys_float) * score_scale
    in_cache = jnp.arange(CACHE_LEN, dtype=jnp.int32)[None, :] < lengths[:, None]
    scores = jnp.where(in_cache[:, None, None, :], scores, -1e+30)
    own_score = jnp.einsum('tkgd,tkd->tkg', query_heads, fresh_heads[:, 0]) * score_scale
    row_max = jnp.maximum(lax.optimization_barrier(jnp.max(scores, -1)), own_score)
    weights_raw = jnp.exp(scores - row_max[..., None])
    own_raw = jnp.exp(own_score - row_max)
    denominator = lax.optimization_barrier(jnp.sum(weights_raw, -1)) + own_raw
    attention_weights = (weights_raw / denominator[..., None]).astype(jnp.bfloat16)
    own_weight = (own_raw / denominator).astype(jnp.bfloat16)
    attended = jnp.einsum('tkgl,tkld->tkgd', attention_weights.astype(jnp.float32), values_float)
    attended = attended + own_weight.astype(jnp.float32)[..., None] * fresh_heads[:, 1][:, :, None, :]
    attended = attended.astype(jnp.bfloat16).reshape(TOKENS, QH * HD)
    projected = jnp.dot(attended, output_weight, preferred_element_type=jnp.float32)
    mixed_rows = residual.astype(jnp.float32) + projected
    normed = (mixed_rows * lax.rsqrt(lax.optimization_barrier(jnp.mean(mixed_rows * mixed_rows, -1, keepdims=True)) + 1e-06) * norm_gain).astype(jnp.bfloat16)
    weights = router_weights / lax.optimization_barrier(jnp.sum(router_weights, -1, keepdims=True))
    flat_experts = routed_experts.reshape(-1)
    most_rows = TOKENS // 4

    def run_expert(expert_index):
        matches = flat_experts == expert_index
        picked = jnp.nonzero(matches, size=most_rows, fill_value=0)[0].astype(jnp.int32)
        is_live = jnp.arange(most_rows, dtype=jnp.int32) < jnp.sum(matches.astype(jnp.int32))
        rows_in = normed[picked // TOPK]
        both_parts = jnp.einsum('nd,gfd->gnf', rows_in.astype(jnp.float32), expert_gate_up[expert_index].astype(jnp.float32))
        hidden_act = (jax.nn.silu(both_parts[0]) * both_parts[1]).astype(jnp.bfloat16)
        expert_rows = jnp.dot(hidden_act, expert_down[expert_index], preferred_element_type=jnp.float32).astype(jnp.bfloat16)
        masked = jnp.where(is_live[:, None], expert_rows.astype(jnp.float32), jnp.zeros((), jnp.float32))
        return (picked, masked)
    picked_all, rows_all = lax.map(run_expert, jnp.arange(EXPERTS, dtype=jnp.int32))
    gathered = jnp.zeros((TOKENS * TOPK, D), jnp.float32).at[picked_all.reshape(-1)].add(rows_all.reshape(-1, D))
    combined = lax.optimization_barrier(jnp.sum(gathered.reshape(TOKENS, TOPK, D) * weights[:, :, None], 1))
    return (mixed_rows + combined).astype(jnp.bfloat16)
```

```python
import functools
import math

import jax
import jax.numpy as jnp
from jax import lax
from jax.experimental import pallas as pl
from jax.experimental.pallas import tpu as pltpu
from jax.sharding import PartitionSpec as P

BF = jnp.bfloat16
F32 = jnp.float32
MESH = pl.DeviceIdType.MESH


def up_to(value, step):
    return -(-value // step) * step


def dot(a, b):
    return jnp.dot(a, b, preferred_element_type=F32)


def dot_nt(a, b):
    return lax.dot_general(a, b, (((1,), (1,)), ((), ())), preferred_element_type=F32)


def layer(
    sizes,
    q_hbm,
    keys_hbm,
    values_hbm,
    fresh_hbm,
    lengths_hbm,
    residual_hbm,
    gain_hbm,
    wo_hbm,
    gate_up_hbm,
    down_hbm,
    routed_hbm,
    router_hbm,
    out_ref,
    q_ref,
    keys_ref,
    values_ref,
    fresh_ref,
    lengths_ref,
    residual_ref,
    gain_ref,
    wo_ref,
    gate_up_ref,
    down_ref,
    routed_ref,
    router_ref,
    att,
    psend,
    prec,
    mixed_ref,
    dsend,
    drecv,
    hbuf,
    rsend,
    rrecv,
    load_sem,
    att_send,
    att_recv,
    p_send,
    p_recv,
    d_send,
    d_recv,
    h_send,
    h_recv,
    r_send,
    r_recv,
):
    wide, narrow, deep = sizes
    experts = wide * deep
    my_wide = lax.axis_index("wide")
    my_narrow = lax.axis_index("narrow")
    my_deep = lax.axis_index("deep")
    my_expert = my_wide * deep + my_deep
    my_quad = my_narrow * deep + my_deep

    rows, local_heads, length, head = keys_ref.shape
    group = q_ref.shape[1] // (local_heads * head)
    width = residual_ref.shape[1]
    part = wo_ref.shape[1]
    share = down_ref.shape[2]
    units = gate_up_ref.shape[2]
    picks = routed_ref.shape[1]
    capacity = rows // 4
    slots = dsend.shape[1] // 2
    half = width // 2
    row_pad = att.shape[2]

    def device(w, n, d):
        return {"wide": w, "narrow": n, "deep": d}

    hbm = (
        q_hbm, fresh_hbm, lengths_hbm, keys_hbm, values_hbm, routed_hbm, router_hbm,
        residual_hbm, gain_hbm, wo_hbm, gate_up_hbm, down_hbm,
    )
    local = (
        q_ref, fresh_ref, lengths_ref, keys_ref, values_ref, routed_ref, router_ref,
        residual_ref, gain_ref, wo_ref, gate_up_ref, down_ref,
    )
    loads = [
        pltpu.make_async_copy(src, dst, load_sem.at[at])
        for at, (src, dst) in enumerate(zip(hbm, local))
    ]
    for load in loads:
        load.start()

    barrier = pltpu.get_barrier_semaphore()
    greeted = 0
    for off in range(1, narrow * deep):
        other = lax.rem(my_quad + off, narrow * deep)
        pl.semaphore_signal(
            barrier, inc=1, device_id=device(my_wide, other // deep, lax.rem(other, deep)),
            device_id_type=MESH,
        )
        greeted += 1
    for w_off in range(1, wide):
        other_wide = lax.rem(my_wide + w_off, wide)
        for d in range(deep):
            pl.semaphore_signal(
                barrier, inc=1, device_id=device(other_wide, my_narrow, d), device_id_type=MESH
            )
            greeted += 1

    for load in loads[:5]:
        load.wait()
    block = 8
    scale = 1.0 / math.sqrt(head)
    lanes = block * length
    lane = lax.broadcasted_iota(jnp.int32, (block, lanes), 1)
    row = lax.broadcasted_iota(jnp.int32, (block, lanes), 0)
    own_block = lane // length == row
    position = lax.rem(lane, length)
    fresh = fresh_ref[...].astype(F32)
    fresh_keys = fresh[:, 0, :]
    fresh_values = fresh[:, 1, :]
    masks = []
    for r in range(rows // block):
        limit = jnp.zeros((block, lanes), jnp.int32)
        for i in range(block):
            limit = jnp.where(row == i, lengths_ref[r * block + i], limit)
        valid = own_block & (position < limit)
        bias = jnp.where(valid, 0.0, -1e30).astype(F32)
        masks.append(jnp.concatenate([bias] * group, 0))
    copies = []
    for k in range(local_heads):
        queries = q_ref[:, k * group * head : (k + 1) * group * head].astype(F32)
        pieces = []
        for r in range(rows // block):
            at = slice(r * block, (r + 1) * block)
            query = jnp.concatenate(
                [queries[at, h * head : (h + 1) * head] for h in range(group)], 0
            )
            keys = keys_ref[at, k].reshape(lanes, head)
            values = values_ref[at, k].reshape(lanes, head)
            new_key = jnp.concatenate([fresh_keys[at, k * head : (k + 1) * head]] * group, 0)
            new_value = jnp.concatenate([fresh_values[at, k * head : (k + 1) * head]] * group, 0)
            keep = masks[r] == 0.0
            scores = jnp.where(keep, dot_nt(query.astype(BF), keys) * scale, -1e30)
            own = jnp.sum(query * new_key, -1, keepdims=True) * scale
            top = jnp.maximum(jnp.max(scores, -1, keepdims=True), own)
            raw = jnp.exp(scores - top)
            own_raw = jnp.exp(own - top)
            total = jnp.sum(raw, -1, keepdims=True) + own_raw
            probs = (raw / total).astype(BF)
            own_prob = (own_raw / total).astype(BF).astype(F32)
            result = dot(probs, values) + own_prob * new_value
            pieces.append(
                jnp.concatenate([result[h * block : (h + 1) * block] for h in range(group)], 1)
            )
        if row_pad > rows:
            pieces.append(jnp.zeros((row_pad - rows, group * head), F32))
        att[k, my_deep] = jnp.concatenate(pieces, 0).astype(BF)
        if k == 0:
            pl.semaphore_wait(barrier, greeted)
        for off in range(1, deep):
            other = lax.rem(my_deep + off, deep)
            copy = pltpu.make_async_remote_copy(
                src_ref=att.at[k, my_deep],
                dst_ref=att.at[k, my_deep],
                send_sem=att_send.at[k, other],
                recv_sem=att_recv.at[k, my_deep],
                device_id=device(my_wide, my_narrow, other),
                device_id_type=MESH,
            )
            copy.start()
            copies.append(copy)

    loads[5].wait()
    loads[6].wait()
    routed = routed_ref[...]
    router = router_ref[...]
    shares = router / jnp.sum(router, -1, keepdims=True)
    wide_slots = experts * 2 * slots
    slot_lane = lax.broadcasted_iota(jnp.int32, (rows, wide_slots), 1)
    lane_expert = slot_lane // (2 * slots)
    lane_place = lax.rem(slot_lane, 2 * slots)
    named = [lane_expert == routed[:, j : j + 1] for j in range(picks)]
    hits = jnp.zeros((rows, wide_slots), F32)
    for j in range(picks):
        hits = hits + jnp.where(named[j], 1.0, 0.0)
    earlier = (
        lax.broadcasted_iota(jnp.int32, (rows, rows), 0)
        > lax.broadcasted_iota(jnp.int32, (rows, rows), 1)
    )
    before = dot(jnp.where(earlier, 1.0, 0.0).astype(BF), hits.astype(BF))
    place = lane_place.astype(F32)
    low = before == place
    high = before + slots == place
    placing_low = jnp.where(low, hits, 0.0)
    placing_high = jnp.where(high, hits, 0.0)

    loads[9].wait()
    acc = None
    for k in range(local_heads):
        for off in range(1, deep):
            other = lax.rem(my_deep + off, deep)
            pltpu.make_async_remote_copy(
                src_ref=att.at[k, other],
                dst_ref=att.at[k, other],
                send_sem=att_send.at[k, other],
                recv_sem=att_recv.at[k, other],
                device_id=device(my_wide, my_narrow, other),
                device_id_type=MESH,
            ).wait_recv()
        term = dot(
            att[k].reshape(deep * row_pad, group * head),
            wo_ref[k * group * head : (k + 1) * group * head, :],
        )
        acc = term if acc is None else acc + term
    for d in range(deep):
        mine = acc[d * row_pad : d * row_pad + rows]
        psend[d] = jnp.concatenate([mine[:, : part // 2], mine[:, part // 2 :]], 0).astype(BF)
    for off in range(1, narrow * deep):
        other = lax.rem(my_quad + off, narrow * deep)
        other_deep = lax.rem(other, deep)
        copy = pltpu.make_async_remote_copy(
            src_ref=psend.at[other_deep],
            dst_ref=prec.at[my_quad],
            send_sem=p_send.at[other],
            recv_sem=p_recv.at[my_quad],
            device_id=device(my_wide, other // deep, other_deep),
            device_id_type=MESH,
        )
        copy.start()
        copies.append(copy)
    prec[my_quad] = psend[my_deep]

    loads[7].wait()
    loads[8].wait()
    for off in range(1, narrow * deep):
        other = lax.rem(my_quad + off, narrow * deep)
        pltpu.make_async_remote_copy(
            src_ref=psend.at[0],
            dst_ref=prec.at[other],
            send_sem=p_send.at[other],
            recv_sem=p_recv.at[other],
            device_id=device(my_wide, other // deep, lax.rem(other, deep)),
            device_id_type=MESH,
        ).wait_recv()
    projected = []
    for d in range(deep):
        total = prec[d].astype(F32)
        for n in range(1, narrow):
            total = total + prec[n * deep + d].astype(F32)
        projected += [total[:rows], total[rows:]]
    mixed = residual_ref[...].astype(F32) + jnp.concatenate(projected, 1)
    mixed_ref[...] = mixed
    squares = jnp.sum(mixed * mixed, -1, keepdims=True)
    normed = (mixed * lax.rsqrt(squares / width + 1e-06) * gain_ref[...]).astype(BF)
    outgoing_low = lax.dot_general(
        placing_low.T.astype(BF), normed[:, :half], (((1,), (0,)), ((), ())),
        preferred_element_type=F32,
    )
    outgoing_high = lax.dot_general(
        placing_high.T.astype(BF), normed[:, half:], (((1,), (0,)), ((), ())),
        preferred_element_type=F32,
    )
    dsend[...] = (outgoing_low + outgoing_high).astype(BF).reshape(experts, 2 * slots, half)
    for off in range(1, experts):
        other = lax.rem(my_expert + off, experts)
        copy = pltpu.make_async_remote_copy(
            src_ref=dsend.at[other],
            dst_ref=drecv.at[my_expert],
            send_sem=d_send.at[other],
            recv_sem=d_recv.at[my_expert],
            device_id=device(other // deep, my_narrow, lax.rem(other, deep)),
            device_id_type=MESH,
        )
        copy.start()
        copies.append(copy)
    drecv[my_expert] = dsend[my_expert]

    loads[10].wait()
    for off in range(1, experts):
        other = lax.rem(my_expert + off, experts)
        pltpu.make_async_remote_copy(
            src_ref=dsend.at[other],
            dst_ref=drecv.at[other],
            send_sem=d_send.at[other],
            recv_sem=d_recv.at[other],
            device_id=device(other // deep, my_narrow, lax.rem(other, deep)),
            device_id_type=MESH,
        ).wait_recv()
    arrived = drecv[...].reshape(experts * 2 * slots, half)
    both = []
    for g in range(2):
        low_part = dot_nt(arrived, gate_up_ref[0, g, :, :half])
        high_part = dot_nt(arrived, gate_up_ref[0, g, :, half:])
        low_part = low_part.reshape(experts, 2 * slots, units)[:, :slots]
        high_part = high_part.reshape(experts, 2 * slots, units)[:, slots:]
        both.append((low_part + high_part).reshape(experts * slots, units))
    hidden = (both[0] / (1.0 + jnp.exp(-both[0])) * both[1]).astype(BF)
    hbuf[my_narrow] = hidden
    for off in range(1, narrow):
        other = lax.rem(my_narrow + off, narrow)
        copy = pltpu.make_async_remote_copy(
            src_ref=hbuf.at[my_narrow],
            dst_ref=hbuf.at[my_narrow],
            send_sem=h_send.at[other],
            recv_sem=h_recv.at[my_narrow],
            device_id=device(my_wide, other, my_deep),
            device_id_type=MESH,
        )
        copy.start()
        copies.append(copy)

    loads[11].wait()

    def down_rows(n):
        return down_ref[0, pl.ds(pl.multiple_of(n * units, units), units), :]

    result = dot(hidden, down_rows(my_narrow))
    for off in range(1, narrow):
        other = lax.rem(my_narrow + off, narrow)
        pltpu.make_async_remote_copy(
            src_ref=hbuf.at[other],
            dst_ref=hbuf.at[other],
            send_sem=h_send.at[other],
            recv_sem=h_recv.at[other],
            device_id=device(my_wide, other, my_deep),
            device_id_type=MESH,
        ).wait_recv()
        result = result + dot(hbuf[other], down_rows(other))
    result = result.reshape(experts, slots, share)
    rsend[...] = jnp.concatenate(
        [result[:, :, : share // 2], result[:, :, share // 2 :]], 1
    ).astype(BF)
    for off in range(1, experts):
        other = lax.rem(my_expert + off, experts)
        copy = pltpu.make_async_remote_copy(
            src_ref=rsend.at[other],
            dst_ref=rrecv.at[my_expert],
            send_sem=r_send.at[other],
            recv_sem=r_recv.at[my_expert],
            device_id=device(other // deep, my_narrow, lax.rem(other, deep)),
            device_id_type=MESH,
        )
        copy.start()
        copies.append(copy)
    rrecv[my_expert] = rsend[my_expert]

    for off in range(1, experts):
        other = lax.rem(my_expert + off, experts)
        pltpu.make_async_remote_copy(
            src_ref=rsend.at[other],
            dst_ref=rrecv.at[other],
            send_sem=r_send.at[other],
            recv_sem=r_recv.at[other],
            device_id=device(other // deep, my_narrow, lax.rem(other, deep)),
            device_id_type=MESH,
        ).wait_recv()
    returned = rrecv[...].reshape(experts * 2 * slots, share // 2)
    sums = []
    for side in (low, high):
        combined = None
        for j in range(picks):
            pick = jnp.where(named[j] & side, 1.0, 0.0).astype(BF)
            term = dot(pick, returned) * shares[:, j : j + 1]
            combined = term if combined is None else combined + term
        sums.append(combined)
    my_columns = pl.ds(pl.multiple_of(my_narrow * share, share), share)
    out_ref[...] = (mixed_ref[:, my_columns] + jnp.concatenate(sums, 1)).astype(BF)
    for copy in copies:
        copy.wait_send()


def shards(sizes, *operands):
    (queries, cache_keys, cache_values, fresh_pairs, lengths, residual, norm_gain,
     output_weight, expert_gate_up, expert_down, routed_experts, router_weights) = operands
    wide, narrow, deep = sizes
    experts = wide * deep
    rows = queries.shape[0]
    local_heads = cache_keys.shape[1]
    width = residual.shape[1]
    part = output_weight.shape[1]
    units = expert_gate_up.shape[2]
    share = expert_down.shape[2]
    slots = up_to(rows // 4, 8)
    operands = (queries, cache_keys, cache_values, fresh_pairs, lengths, residual,
                norm_gain.reshape(1, width), output_weight, expert_gate_up, expert_down,
                routed_experts, router_weights)
    dma = pltpu.SemaphoreType.DMA
    held = [
        pltpu.SMEM(x.shape, x.dtype) if x is lengths else pltpu.VMEM(x.shape, x.dtype)
        for x in operands
    ]
    return pl.pallas_call(
        functools.partial(layer, sizes),
        out_shape=jax.ShapeDtypeStruct((rows, share), BF),
        in_specs=[pl.BlockSpec(memory_space=pl.ANY)] * len(operands),
        out_specs=pl.BlockSpec(memory_space=pltpu.VMEM),
        scratch_shapes=held
        + [
            pltpu.VMEM((local_heads, deep, up_to(rows, 16), queries.shape[1] // local_heads), BF),
            pltpu.VMEM((deep, 2 * rows, part // 2), BF),
            pltpu.VMEM((narrow * deep, 2 * rows, part // 2), BF),
            pltpu.VMEM((rows, width), F32),
            pltpu.VMEM((experts, 2 * slots, width // 2), BF),
            pltpu.VMEM((experts, 2 * slots, width // 2), BF),
            pltpu.VMEM((narrow, experts * slots, units), BF),
            pltpu.VMEM((experts, 2 * slots, share // 2), BF),
            pltpu.VMEM((experts, 2 * slots, share // 2), BF),
            dma((len(operands),)),
            dma((local_heads, deep)),
            dma((local_heads, deep)),
            dma((narrow * deep,)),
            dma((narrow * deep,)),
            dma((experts,)),
            dma((experts,)),
            dma((narrow,)),
            dma((narrow,)),
            dma((experts,)),
            dma((experts,)),
        ],
        compiler_params=pltpu.CompilerParams(
            collective_id=0, has_side_effects=True, vmem_limit_bytes=48 * 1024 * 1024
        ),
    )(*operands)


def solution(mesh):
    in_specs = (
        P(("group", "wide", "deep"), "narrow"),
        P(("group", "wide", "deep"), "narrow", None, None),
        P(("group", "wide", "deep"), "narrow", None, None),
        P(("group", "wide", "deep"), None, "narrow"),
        P(("group", "wide", "deep")),
        P(("group", "wide", "deep"), None),
        P(),
        P("narrow", "deep"),
        P(("wide", "deep"), None, "narrow", None),
        P(("wide", "deep"), None, "narrow"),
        P(("group", "wide", "deep"), None),
        P(("group", "wide", "deep"), None),
    )
    out_specs = P(("group", "wide", "deep"), "narrow")
    sizes = (mesh.shape["wide"], mesh.shape["narrow"], mesh.shape["deep"])
    return jax.shard_map(
        functools.partial(shards, sizes), mesh=mesh, in_specs=in_specs, out_specs=out_specs,
        check_vma=False,
    )
```

```python
import functools
import math

import jax
import jax.numpy as jnp
from jax import lax
from jax.experimental import pallas as pl
from jax.experimental.pallas import tpu as pltpu
from jax.sharding import PartitionSpec as P

BF = jnp.bfloat16
F32 = jnp.float32
MESH = pl.DeviceIdType.MESH


def up_to(value, step):
    return -(-value // step) * step


def dot(a, b):
    return jnp.dot(a, b, preferred_element_type=F32)


def dot_nt(a, b):
    return lax.dot_general(a, b, (((1,), (1,)), ((), ())), preferred_element_type=F32)


def layer(
    sizes,
    q_hbm,
    keys_hbm,
    values_hbm,
    fresh_hbm,
    lengths_hbm,
    residual_hbm,
    gain_hbm,
    wo_hbm,
    gate_up_hbm,
    down_hbm,
    routed_hbm,
    router_hbm,
    out_ref,
    q_ref,
    keys_ref,
    values_ref,
    fresh_ref,
    lengths_ref,
    residual_ref,
    gain_ref,
    wo_ref,
    gate_up_ref,
    down_ref,
    routed_ref,
    router_ref,
    att,
    psend,
    prec,
    mixed_ref,
    dsend,
    drecv,
    hbuf,
    rsend,
    rrecv,
    load_sem,
    att_send,
    att_recv,
    p_send,
    p_recv,
    d_send,
    d_recv,
    h_send,
    h_recv,
    r_send,
    r_recv,
):
    wide, narrow, deep = sizes
    experts = wide * deep
    my_wide = lax.axis_index("wide")
    my_narrow = lax.axis_index("narrow")
    my_deep = lax.axis_index("deep")
    my_expert = my_wide * deep + my_deep
    my_quad = my_narrow * deep + my_deep

    rows, local_heads, length, head = keys_ref.shape
    group = q_ref.shape[1] // (local_heads * head)
    width = residual_ref.shape[1]
    part = wo_ref.shape[1]
    share = down_ref.shape[2]
    units = gate_up_ref.shape[2]
    picks = routed_ref.shape[0]
    capacity = rows // 4
    slots = dsend.shape[1] // 2
    half = width // 2
    row_pad = att.shape[2]

    def device(w, n, d):
        return {"wide": w, "narrow": n, "deep": d}

    hbm = (
        q_hbm, fresh_hbm, lengths_hbm, keys_hbm, values_hbm, routed_hbm, router_hbm,
        residual_hbm, gain_hbm, wo_hbm, gate_up_hbm, down_hbm,
    )
    local = (
        q_ref, fresh_ref, lengths_ref, keys_ref, values_ref, routed_ref, router_ref,
        residual_ref, gain_ref, wo_ref, gate_up_ref, down_ref,
    )
    loads = [
        pltpu.make_async_copy(src, dst, load_sem.at[at])
        for at, (src, dst) in enumerate(zip(hbm, local))
    ]
    for load in loads:
        load.start()

    barrier = pltpu.get_barrier_semaphore()
    greeted = 0
    for off in range(1, narrow * deep):
        other = lax.rem(my_quad + off, narrow * deep)
        pl.semaphore_signal(
            barrier, inc=1, device_id=device(my_wide, other // deep, lax.rem(other, deep)),
            device_id_type=MESH,
        )
        greeted += 1
    for w_off in range(1, wide):
        other_wide = lax.rem(my_wide + w_off, wide)
        for d in range(deep):
            pl.semaphore_signal(
                barrier, inc=1, device_id=device(other_wide, my_narrow, d), device_id_type=MESH
            )
            greeted += 1

    for load in loads[:5]:
        load.wait()
    block = 8
    scale = 1.0 / math.sqrt(head)
    lanes = block * length
    lane = lax.broadcasted_iota(jnp.int32, (block, lanes), 1)
    row = lax.broadcasted_iota(jnp.int32, (block, lanes), 0)
    own_block = lane // length == row
    position = lax.rem(lane, length)
    fresh = fresh_ref[...].astype(F32)
    fresh_keys = fresh[:, 0, :]
    fresh_values = fresh[:, 1, :]
    masks = []
    for r in range(rows // block):
        limit = jnp.zeros((block, lanes), jnp.int32)
        for i in range(block):
            limit = jnp.where(row == i, lengths_ref[r * block + i], limit)
        valid = own_block & (position < limit)
        bias = jnp.where(valid, 0.0, -1e30).astype(F32)
        masks.append(jnp.concatenate([bias] * group, 0))
    copies = []
    for k in range(local_heads):
        queries = q_ref[:, k * group * head : (k + 1) * group * head].astype(F32)
        pieces = []
        for r in range(rows // block):
            at = slice(r * block, (r + 1) * block)
            query = jnp.concatenate(
                [queries[at, h * head : (h + 1) * head] for h in range(group)], 0
            )
            keys = keys_ref[at, k].reshape(lanes, head)
            values = values_ref[at, k].reshape(lanes, head)
            new_key = jnp.concatenate([fresh_keys[at, k * head : (k + 1) * head]] * group, 0)
            new_value = jnp.concatenate([fresh_values[at, k * head : (k + 1) * head]] * group, 0)
            keep = masks[r] == 0.0
            scores = jnp.where(keep, dot_nt(query.astype(BF), keys) * scale, -1e30)
            own = jnp.sum(query * new_key, -1, keepdims=True) * scale
            top = jnp.maximum(jnp.max(scores, -1, keepdims=True), own)
            raw = jnp.exp(scores - top)
            own_raw = jnp.exp(own - top)
            total = jnp.sum(raw, -1, keepdims=True) + own_raw
            probs = (raw / total).astype(BF)
            own_prob = (own_raw / total).astype(BF).astype(F32)
            result = dot(probs, values) + own_prob * new_value
            pieces.append(
                jnp.concatenate([result[h * block : (h + 1) * block] for h in range(group)], 1)
            )
        if row_pad > rows:
            pieces.append(jnp.zeros((row_pad - rows, group * head), F32))
        att[k, my_deep] = jnp.concatenate(pieces, 0).astype(BF)
        if k == 0:
            pl.semaphore_wait(barrier, greeted)
        for off in range(1, deep):
            other = lax.rem(my_deep + off, deep)
            copy = pltpu.make_async_remote_copy(
                src_ref=att.at[k, my_deep],
                dst_ref=att.at[k, my_deep],
                send_sem=att_send.at[k, other],
                recv_sem=att_recv.at[k, my_deep],
                device_id=device(my_wide, my_narrow, other),
                device_id_type=MESH,
            )
            copy.start()
            copies.append(copy)

    loads[5].wait()
    loads[6].wait()
    square = (rows, rows)
    down_at = lax.broadcasted_iota(jnp.int32, square, 0)
    across_at = lax.broadcasted_iota(jnp.int32, square, 1)

    def column(line):
        spread = jnp.where(down_at == across_at, line, jnp.zeros_like(line))
        return jnp.sum(spread, -1, keepdims=True)

    router = router_ref[...]
    shares = router / jnp.sum(router, 0, keepdims=True)
    shares = [column(shares[j : j + 1, :]) for j in range(picks)]
    routed = [column(routed_ref[j : j + 1, :]) for j in range(picks)]
    wide_slots = experts * 2 * slots
    slot_lane = lax.broadcasted_iota(jnp.int32, (rows, wide_slots), 1)
    lane_expert = slot_lane // (2 * slots)
    lane_place = lax.rem(slot_lane, 2 * slots)
    named = [lane_expert == routed[j] for j in range(picks)]
    hits = jnp.zeros((rows, wide_slots), F32)
    for j in range(picks):
        hits = hits + jnp.where(named[j], 1.0, 0.0)
    before = dot(jnp.where(down_at > across_at, 1.0, 0.0).astype(BF), hits.astype(BF))
    place = lane_place.astype(F32)
    low = before == place
    high = before + slots == place
    placing_low = jnp.where(low, hits, 0.0)
    placing_high = jnp.where(high, hits, 0.0)

    loads[9].wait()
    acc = None
    for k in range(local_heads):
        for off in range(1, deep):
            other = lax.rem(my_deep + off, deep)
            pltpu.make_async_remote_copy(
                src_ref=att.at[k, other],
                dst_ref=att.at[k, other],
                send_sem=att_send.at[k, other],
                recv_sem=att_recv.at[k, other],
                device_id=device(my_wide, my_narrow, other),
                device_id_type=MESH,
            ).wait_recv()
        term = dot(
            att[k].reshape(deep * row_pad, group * head),
            wo_ref[k * group * head : (k + 1) * group * head, :],
        )
        acc = term if acc is None else acc + term
    for d in range(deep):
        mine = acc[d * row_pad : d * row_pad + rows]
        psend[d] = jnp.concatenate([mine[:, : part // 2], mine[:, part // 2 :]], 0).astype(BF)
    for off in range(1, narrow * deep):
        other = lax.rem(my_quad + off, narrow * deep)
        other_deep = lax.rem(other, deep)
        copy = pltpu.make_async_remote_copy(
            src_ref=psend.at[other_deep],
            dst_ref=prec.at[my_quad],
            send_sem=p_send.at[other],
            recv_sem=p_recv.at[my_quad],
            device_id=device(my_wide, other // deep, other_deep),
            device_id_type=MESH,
        )
        copy.start()
        copies.append(copy)
    prec[my_quad] = psend[my_deep]

    loads[7].wait()
    loads[8].wait()
    for off in range(1, narrow * deep):
        other = lax.rem(my_quad + off, narrow * deep)
        pltpu.make_async_remote_copy(
            src_ref=psend.at[0],
            dst_ref=prec.at[other],
            send_sem=p_send.at[other],
            recv_sem=p_recv.at[other],
            device_id=device(my_wide, other // deep, lax.rem(other, deep)),
            device_id_type=MESH,
        ).wait_recv()
    projected = []
    for d in range(deep):
        total = prec[d].astype(F32)
        for n in range(1, narrow):
            total = total + prec[n * deep + d].astype(F32)
        projected += [total[:rows], total[rows:]]
    mixed = residual_ref[...].astype(F32) + jnp.concatenate(projected, 1)
    mixed_ref[...] = mixed
    squares = jnp.sum(mixed * mixed, -1, keepdims=True)
    normed = (mixed * lax.rsqrt(squares / width + 1e-06) * gain_ref[...]).astype(BF)
    outgoing_low = lax.dot_general(
        placing_low.T.astype(BF), normed[:, :half], (((1,), (0,)), ((), ())),
        preferred_element_type=F32,
    )
    outgoing_high = lax.dot_general(
        placing_high.T.astype(BF), normed[:, half:], (((1,), (0,)), ((), ())),
        preferred_element_type=F32,
    )
    dsend[...] = (outgoing_low + outgoing_high).astype(BF).reshape(experts, 2 * slots, half)
    for off in range(1, experts):
        other = lax.rem(my_expert + off, experts)
        copy = pltpu.make_async_remote_copy(
            src_ref=dsend.at[other],
            dst_ref=drecv.at[my_expert],
            send_sem=d_send.at[other],
            recv_sem=d_recv.at[my_expert],
            device_id=device(other // deep, my_narrow, lax.rem(other, deep)),
            device_id_type=MESH,
        )
        copy.start()
        copies.append(copy)
    drecv[my_expert] = dsend[my_expert]

    loads[10].wait()
    for off in range(1, experts):
        other = lax.rem(my_expert + off, experts)
        pltpu.make_async_remote_copy(
            src_ref=dsend.at[other],
            dst_ref=drecv.at[other],
            send_sem=d_send.at[other],
            recv_sem=d_recv.at[other],
            device_id=device(other // deep, my_narrow, lax.rem(other, deep)),
            device_id_type=MESH,
        ).wait_recv()
    arrived = drecv[...].reshape(experts * 2 * slots, half)
    both = []
    for g in range(2):
        low_part = dot_nt(arrived, gate_up_ref[0, g, :, :half])
        high_part = dot_nt(arrived, gate_up_ref[0, g, :, half:])
        low_part = low_part.reshape(experts, 2 * slots, units)[:, :slots]
        high_part = high_part.reshape(experts, 2 * slots, units)[:, slots:]
        both.append((low_part + high_part).reshape(experts * slots, units))
    hidden = (both[0] / (1.0 + jnp.exp(-both[0])) * both[1]).astype(BF)
    hbuf[my_narrow] = hidden
    for off in range(1, narrow):
        other = lax.rem(my_narrow + off, narrow)
        copy = pltpu.make_async_remote_copy(
            src_ref=hbuf.at[my_narrow],
            dst_ref=hbuf.at[my_narrow],
            send_sem=h_send.at[other],
            recv_sem=h_recv.at[my_narrow],
            device_id=device(my_wide, other, my_deep),
            device_id_type=MESH,
        )
        copy.start()
        copies.append(copy)

    loads[11].wait()

    def down_rows(n):
        return down_ref[0, pl.ds(pl.multiple_of(n * units, units), units), :]

    result = dot(hidden, down_rows(my_narrow))
    for off in range(1, narrow):
        other = lax.rem(my_narrow + off, narrow)
        pltpu.make_async_remote_copy(
            src_ref=hbuf.at[other],
            dst_ref=hbuf.at[other],
            send_sem=h_send.at[other],
            recv_sem=h_recv.at[other],
            device_id=device(my_wide, other, my_deep),
            device_id_type=MESH,
        ).wait_recv()
        result = result + dot(hbuf[other], down_rows(other))
    result = result.reshape(experts, slots, share)
    rsend[...] = jnp.concatenate(
        [result[:, :, : share // 2], result[:, :, share // 2 :]], 1
    ).astype(BF)
    for off in range(1, experts):
        other = lax.rem(my_expert + off, experts)
        copy = pltpu.make_async_remote_copy(
            src_ref=rsend.at[other],
            dst_ref=rrecv.at[my_expert],
            send_sem=r_send.at[other],
            recv_sem=r_recv.at[my_expert],
            device_id=device(other // deep, my_narrow, lax.rem(other, deep)),
            device_id_type=MESH,
        )
        copy.start()
        copies.append(copy)
    rrecv[my_expert] = rsend[my_expert]

    for off in range(1, experts):
        other = lax.rem(my_expert + off, experts)
        pltpu.make_async_remote_copy(
            src_ref=rsend.at[other],
            dst_ref=rrecv.at[other],
            send_sem=r_send.at[other],
            recv_sem=r_recv.at[other],
            device_id=device(other // deep, my_narrow, lax.rem(other, deep)),
            device_id_type=MESH,
        ).wait_recv()
    returned = rrecv[...].reshape(experts * 2 * slots, share // 2)
    sums = []
    for side in (low, high):
        combined = None
        for j in range(picks):
            pick = jnp.where(named[j] & side, 1.0, 0.0).astype(BF)
            term = dot(pick, returned) * shares[j]
            combined = term if combined is None else combined + term
        sums.append(combined)
    my_columns = pl.ds(pl.multiple_of(my_narrow * share, share), share)
    out_ref[...] = (mixed_ref[:, my_columns] + jnp.concatenate(sums, 1)).astype(BF)
    for copy in copies:
        copy.wait_send()


def shards(sizes, *operands):
    (queries, cache_keys, cache_values, fresh_pairs, lengths, residual, norm_gain,
     output_weight, expert_gate_up, expert_down, routed_experts, router_weights) = operands
    wide, narrow, deep = sizes
    experts = wide * deep
    rows = queries.shape[0]
    local_heads = cache_keys.shape[1]
    width = residual.shape[1]
    part = output_weight.shape[1]
    units = expert_gate_up.shape[2]
    share = expert_down.shape[2]
    slots = up_to(rows // 4, 8)
    operands = (queries, cache_keys, cache_values, fresh_pairs, lengths, residual,
                norm_gain.reshape(1, width), output_weight, expert_gate_up, expert_down,
                routed_experts.T, router_weights.T)
    dma = pltpu.SemaphoreType.DMA
    held = [
        pltpu.SMEM(x.shape, x.dtype) if x is lengths else pltpu.VMEM(x.shape, x.dtype)
        for x in operands
    ]
    return pl.pallas_call(
        functools.partial(layer, sizes),
        out_shape=jax.ShapeDtypeStruct((rows, share), BF),
        in_specs=[pl.BlockSpec(memory_space=pl.ANY)] * len(operands),
        out_specs=pl.BlockSpec(memory_space=pltpu.VMEM),
        scratch_shapes=held
        + [
            pltpu.VMEM((local_heads, deep, up_to(rows, 16), queries.shape[1] // local_heads), BF),
            pltpu.VMEM((deep, 2 * rows, part // 2), BF),
            pltpu.VMEM((narrow * deep, 2 * rows, part // 2), BF),
            pltpu.VMEM((rows, width), F32),
            pltpu.VMEM((experts, 2 * slots, width // 2), BF),
            pltpu.VMEM((experts, 2 * slots, width // 2), BF),
            pltpu.VMEM((narrow, experts * slots, units), BF),
            pltpu.VMEM((experts, 2 * slots, share // 2), BF),
            pltpu.VMEM((experts, 2 * slots, share // 2), BF),
            dma((len(operands),)),
            dma((local_heads, deep)),
            dma((local_heads, deep)),
            dma((narrow * deep,)),
            dma((narrow * deep,)),
            dma((experts,)),
            dma((experts,)),
            dma((narrow,)),
            dma((narrow,)),
            dma((experts,)),
            dma((experts,)),
        ],
        compiler_params=pltpu.CompilerParams(
            collective_id=0, has_side_effects=True, vmem_limit_bytes=63 * 1024 * 1024
        ),
    )(*operands)


def solution(mesh):
    in_specs = (
        P(("group", "wide", "deep"), "narrow"),
        P(("group", "wide", "deep"), "narrow", None, None),
        P(("group", "wide", "deep"), "narrow", None, None),
        P(("group", "wide", "deep"), None, "narrow"),
        P(("group", "wide", "deep")),
        P(("group", "wide", "deep"), None),
        P(),
        P("narrow", "deep"),
        P(("wide", "deep"), None, "narrow", None),
        P(("wide", "deep"), None, "narrow"),
        P(("group", "wide", "deep"), None),
        P(("group", "wide", "deep"), None),
    )
    out_specs = P(("group", "wide", "deep"), "narrow")
    sizes = (mesh.shape["wide"], mesh.shape["narrow"], mesh.shape["deep"])
    return jax.shard_map(
        functools.partial(shards, sizes), mesh=mesh, in_specs=in_specs, out_specs=out_specs,
        check_vma=False,
    )
```

```python
import functools
import math

import jax
import jax.numpy as jnp
from jax import lax
from jax.experimental import pallas as pl
from jax.experimental.pallas import tpu as pltpu
from jax.sharding import PartitionSpec as P

BF = jnp.bfloat16
F32 = jnp.float32
MESH = pl.DeviceIdType.MESH


def up_to(value, step):
    return -(-value // step) * step


def dot(a, b):
    return jnp.dot(a, b, preferred_element_type=F32)


def dot_nt(a, b):
    return lax.dot_general(a, b, (((1,), (1,)), ((), ())), preferred_element_type=F32)


def layer(
    sizes,
    q_hbm,
    keys_hbm,
    values_hbm,
    fresh_hbm,
    lengths_hbm,
    residual_hbm,
    gain_hbm,
    wo_hbm,
    gate_up_hbm,
    down_hbm,
    routed_hbm,
    router_hbm,
    out_ref,
    q_ref,
    keys_ref,
    values_ref,
    fresh_ref,
    lengths_ref,
    residual_ref,
    gain_ref,
    wo_ref,
    gate_up_ref,
    down_ref,
    routed_ref,
    router_ref,
    att,
    psend,
    prec,
    mixed_ref,
    dsend,
    drecv,
    hbuf,
    rsend,
    rrecv,
    load_sem,
    att_send,
    att_recv,
    p_send,
    p_recv,
    d_send,
    d_recv,
    h_send,
    h_recv,
    r_send,
    r_recv,
):
    wide, narrow, deep = sizes
    experts = wide * deep
    my_wide = lax.axis_index("wide")
    my_narrow = lax.axis_index("narrow")
    my_deep = lax.axis_index("deep")
    my_expert = my_wide * deep + my_deep
    my_quad = my_narrow * deep + my_deep

    rows, local_heads, length, head = keys_ref.shape
    group = q_ref.shape[1] // (local_heads * head)
    width = residual_ref.shape[1]
    part = wo_ref.shape[1]
    share = down_ref.shape[2]
    units = gate_up_ref.shape[2]
    picks = routed_ref.shape[0]
    capacity = rows // 4
    slots = dsend.shape[1] // 2
    half = width // 2
    row_pad = att.shape[2]

    def device(w, n, d):
        return {"wide": w, "narrow": n, "deep": d}

    far_first = sorted(range(1, experts), key=lambda off: abs(2 * off - experts))

    hbm = (
        q_hbm, fresh_hbm, lengths_hbm, keys_hbm, values_hbm, routed_hbm, router_hbm,
        residual_hbm, gain_hbm, wo_hbm, gate_up_hbm, down_hbm,
    )
    local = (
        q_ref, fresh_ref, lengths_ref, keys_ref, values_ref, routed_ref, router_ref,
        residual_ref, gain_ref, wo_ref, gate_up_ref, down_ref,
    )
    loads = [
        pltpu.make_async_copy(src, dst, load_sem.at[at])
        for at, (src, dst) in enumerate(zip(hbm, local))
    ]
    for load in loads:
        load.start()

    barrier = pltpu.get_barrier_semaphore()
    greeted = 0
    for off in range(1, narrow * deep):
        other = lax.rem(my_quad + off, narrow * deep)
        pl.semaphore_signal(
            barrier, inc=1, device_id=device(my_wide, other // deep, lax.rem(other, deep)),
            device_id_type=MESH,
        )
        greeted += 1
    for w_off in range(1, wide):
        other_wide = lax.rem(my_wide + w_off, wide)
        for d in range(deep):
            pl.semaphore_signal(
                barrier, inc=1, device_id=device(other_wide, my_narrow, d), device_id_type=MESH
            )
            greeted += 1

    for load in loads[:5]:
        load.wait()
    block = 8
    scale = 1.0 / math.sqrt(head)
    lanes = block * length
    lane = lax.broadcasted_iota(jnp.int32, (block, lanes), 1)
    row = lax.broadcasted_iota(jnp.int32, (block, lanes), 0)
    own_block = lane // length == row
    position = lax.rem(lane, length)
    fresh = fresh_ref[...].astype(F32)
    fresh_keys = fresh[:, 0, :]
    fresh_values = fresh[:, 1, :]
    masks = []
    for r in range(rows // block):
        limit = jnp.zeros((block, lanes), jnp.int32)
        for i in range(block):
            limit = jnp.where(row == i, lengths_ref[r * block + i], limit)
        valid = own_block & (position < limit)
        bias = jnp.where(valid, 0.0, -1e30).astype(F32)
        masks.append(jnp.concatenate([bias] * group, 0))
    for k in range(local_heads):
        queries = q_ref[:, k * group * head : (k + 1) * group * head].astype(F32)
        pieces = []
        for r in range(rows // block):
            at = slice(r * block, (r + 1) * block)
            query = jnp.concatenate(
                [queries[at, h * head : (h + 1) * head] for h in range(group)], 0
            )
            keys = keys_ref[at, k].reshape(lanes, head)
            values = values_ref[at, k].reshape(lanes, head)
            new_key = jnp.concatenate([fresh_keys[at, k * head : (k + 1) * head]] * group, 0)
            new_value = jnp.concatenate([fresh_values[at, k * head : (k + 1) * head]] * group, 0)
            keep = masks[r] == 0.0
            scores = jnp.where(keep, dot_nt(query.astype(BF), keys) * scale, -1e30)
            own = jnp.sum(query * new_key, -1, keepdims=True) * scale
            top = jnp.maximum(jnp.max(scores, -1, keepdims=True), own)
            raw = jnp.exp(scores - top)
            own_raw = jnp.exp(own - top)
            total = jnp.sum(raw, -1, keepdims=True) + own_raw
            probs = (raw / total).astype(BF)
            own_prob = (own_raw / total).astype(BF).astype(F32)
            result = dot(probs, values) + own_prob * new_value
            pieces.append(
                jnp.concatenate([result[h * block : (h + 1) * block] for h in range(group)], 1)
            )
        if row_pad > rows:
            pieces.append(jnp.zeros((row_pad - rows, group * head), F32))
        att[k, my_deep] = jnp.concatenate(pieces, 0).astype(BF)

    loads[5].wait()
    loads[6].wait()
    square = (rows, rows)
    down_at = lax.broadcasted_iota(jnp.int32, square, 0)
    across_at = lax.broadcasted_iota(jnp.int32, square, 1)

    def column(line):
        spread = jnp.where(down_at == across_at, line, jnp.zeros_like(line))
        return jnp.sum(spread, -1, keepdims=True)

    router = router_ref[...]
    shares = router / jnp.sum(router, 0, keepdims=True)
    shares = [column(shares[j : j + 1, :]) for j in range(picks)]
    routed = [column(routed_ref[j : j + 1, :]) for j in range(picks)]
    wide_slots = experts * 2 * slots
    slot_lane = lax.broadcasted_iota(jnp.int32, (rows, wide_slots), 1)
    lane_expert = slot_lane // (2 * slots)
    lane_place = lax.rem(slot_lane, 2 * slots)
    named = [lane_expert == routed[j] for j in range(picks)]
    hits = jnp.zeros((rows, wide_slots), F32)
    for j in range(picks):
        hits = hits + jnp.where(named[j], 1.0, 0.0)
    before = dot(jnp.where(down_at > across_at, 1.0, 0.0).astype(BF), hits.astype(BF))
    place = lane_place.astype(F32)
    low = before == place
    high = before + slots == place
    placing_low = jnp.where(low, hits, 0.0)
    placing_high = jnp.where(high, hits, 0.0)

    pl.semaphore_wait(barrier, greeted)
    copies = []
    for k in range(local_heads):
        for off in range(1, deep):
            other = lax.rem(my_deep + off, deep)
            copy = pltpu.make_async_remote_copy(
                src_ref=att.at[k, my_deep],
                dst_ref=att.at[k, my_deep],
                send_sem=att_send.at[k, other],
                recv_sem=att_recv.at[k, my_deep],
                device_id=device(my_wide, my_narrow, other),
                device_id_type=MESH,
            )
            copy.start()
            copies.append(copy)

    loads[9].wait()
    acc = None
    for k in range(local_heads):
        for off in range(1, deep):
            other = lax.rem(my_deep + off, deep)
            pltpu.make_async_remote_copy(
                src_ref=att.at[k, other],
                dst_ref=att.at[k, other],
                send_sem=att_send.at[k, other],
                recv_sem=att_recv.at[k, other],
                device_id=device(my_wide, my_narrow, other),
                device_id_type=MESH,
            ).wait_recv()
        term = dot(
            att[k].reshape(deep * row_pad, group * head),
            wo_ref[k * group * head : (k + 1) * group * head, :],
        )
        acc = term if acc is None else acc + term
    for d in range(deep):
        mine = acc[d * row_pad : d * row_pad + rows]
        psend[d] = jnp.concatenate([mine[:, : part // 2], mine[:, part // 2 :]], 0).astype(BF)
    for off in range(1, narrow * deep):
        other = lax.rem(my_quad + off, narrow * deep)
        other_deep = lax.rem(other, deep)
        copy = pltpu.make_async_remote_copy(
            src_ref=psend.at[other_deep],
            dst_ref=prec.at[my_quad],
            send_sem=p_send.at[other],
            recv_sem=p_recv.at[my_quad],
            device_id=device(my_wide, other // deep, other_deep),
            device_id_type=MESH,
        )
        copy.start()
        copies.append(copy)
    prec[my_quad] = psend[my_deep]

    loads[7].wait()
    loads[8].wait()
    for off in range(1, narrow * deep):
        other = lax.rem(my_quad + off, narrow * deep)
        pltpu.make_async_remote_copy(
            src_ref=psend.at[0],
            dst_ref=prec.at[other],
            send_sem=p_send.at[other],
            recv_sem=p_recv.at[other],
            device_id=device(my_wide, other // deep, lax.rem(other, deep)),
            device_id_type=MESH,
        ).wait_recv()
    projected = []
    for d in range(deep):
        total = prec[d].astype(F32)
        for n in range(1, narrow):
            total = total + prec[n * deep + d].astype(F32)
        projected += [total[:rows], total[rows:]]
    mixed = residual_ref[...].astype(F32) + jnp.concatenate(projected, 1)
    mixed_ref[...] = mixed
    squares = jnp.sum(mixed * mixed, -1, keepdims=True)
    normed = (mixed * lax.rsqrt(squares / width + 1e-06) * gain_ref[...]).astype(BF)
    outgoing_low = lax.dot_general(
        placing_low.T.astype(BF), normed[:, :half], (((1,), (0,)), ((), ())),
        preferred_element_type=F32,
    )
    outgoing_high = lax.dot_general(
        placing_high.T.astype(BF), normed[:, half:], (((1,), (0,)), ((), ())),
        preferred_element_type=F32,
    )
    dsend[...] = (outgoing_low + outgoing_high).astype(BF).reshape(experts, 2 * slots, half)
    for off in far_first:
        other = lax.rem(my_expert + off, experts)
        copy = pltpu.make_async_remote_copy(
            src_ref=dsend.at[other],
            dst_ref=drecv.at[my_expert],
            send_sem=d_send.at[other],
            recv_sem=d_recv.at[my_expert],
            device_id=device(other // deep, my_narrow, lax.rem(other, deep)),
            device_id_type=MESH,
        )
        copy.start()
        copies.append(copy)
    drecv[my_expert] = dsend[my_expert]

    loads[10].wait()
    for off in far_first:
        other = lax.rem(my_expert + off, experts)
        pltpu.make_async_remote_copy(
            src_ref=dsend.at[other],
            dst_ref=drecv.at[other],
            send_sem=d_send.at[other],
            recv_sem=d_recv.at[other],
            device_id=device(other // deep, my_narrow, lax.rem(other, deep)),
            device_id_type=MESH,
        ).wait_recv()
    arrived = drecv[...].reshape(experts * 2 * slots, half)
    both = []
    for g in range(2):
        low_part = dot_nt(arrived, gate_up_ref[0, g, :, :half])
        high_part = dot_nt(arrived, gate_up_ref[0, g, :, half:])
        low_part = low_part.reshape(experts, 2 * slots, units)[:, :slots]
        high_part = high_part.reshape(experts, 2 * slots, units)[:, slots:]
        both.append((low_part + high_part).reshape(experts * slots, units))
    hidden = (both[0] / (1.0 + jnp.exp(-both[0])) * both[1]).astype(BF)
    hbuf[my_narrow] = hidden
    for off in range(1, narrow):
        other = lax.rem(my_narrow + off, narrow)
        copy = pltpu.make_async_remote_copy(
            src_ref=hbuf.at[my_narrow],
            dst_ref=hbuf.at[my_narrow],
            send_sem=h_send.at[other],
            recv_sem=h_recv.at[my_narrow],
            device_id=device(my_wide, other, my_deep),
            device_id_type=MESH,
        )
        copy.start()
        copies.append(copy)

    loads[11].wait()

    def down_rows(n):
        return down_ref[0, pl.ds(pl.multiple_of(n * units, units), units), :]

    result = dot(hidden, down_rows(my_narrow))
    for off in range(1, narrow):
        other = lax.rem(my_narrow + off, narrow)
        pltpu.make_async_remote_copy(
            src_ref=hbuf.at[other],
            dst_ref=hbuf.at[other],
            send_sem=h_send.at[other],
            recv_sem=h_recv.at[other],
            device_id=device(my_wide, other, my_deep),
            device_id_type=MESH,
        ).wait_recv()
        result = result + dot(hbuf[other], down_rows(other))
    result = result.reshape(experts, slots, share)
    rsend[...] = jnp.concatenate(
        [result[:, :, : share // 2], result[:, :, share // 2 :]], 1
    ).astype(BF)
    for off in far_first:
        other = lax.rem(my_expert + off, experts)
        copy = pltpu.make_async_remote_copy(
            src_ref=rsend.at[other],
            dst_ref=rrecv.at[my_expert],
            send_sem=r_send.at[other],
            recv_sem=r_recv.at[my_expert],
            device_id=device(other // deep, my_narrow, lax.rem(other, deep)),
            device_id_type=MESH,
        )
        copy.start()
        copies.append(copy)
    rrecv[my_expert] = rsend[my_expert]

    for off in far_first:
        other = lax.rem(my_expert + off, experts)
        pltpu.make_async_remote_copy(
            src_ref=rsend.at[other],
            dst_ref=rrecv.at[other],
            send_sem=r_send.at[other],
            recv_sem=r_recv.at[other],
            device_id=device(other // deep, my_narrow, lax.rem(other, deep)),
            device_id_type=MESH,
        ).wait_recv()
    returned = rrecv[...].reshape(experts * 2 * slots, share // 2)
    sums = []
    for side in (low, high):
        combined = None
        for j in range(picks):
            pick = jnp.where(named[j] & side, 1.0, 0.0).astype(BF)
            term = dot(pick, returned) * shares[j]
            combined = term if combined is None else combined + term
        sums.append(combined)
    my_columns = pl.ds(pl.multiple_of(my_narrow * share, share), share)
    out_ref[...] = (mixed_ref[:, my_columns] + jnp.concatenate(sums, 1)).astype(BF)
    for copy in copies:
        copy.wait_send()


def shards(sizes, *operands):
    (queries, cache_keys, cache_values, fresh_pairs, lengths, residual, norm_gain,
     output_weight, expert_gate_up, expert_down, routed_experts, router_weights) = operands
    wide, narrow, deep = sizes
    experts = wide * deep
    rows = queries.shape[0]
    local_heads = cache_keys.shape[1]
    width = residual.shape[1]
    part = output_weight.shape[1]
    units = expert_gate_up.shape[2]
    share = expert_down.shape[2]
    slots = up_to(rows // 4, 8)
    operands = (queries, cache_keys, cache_values, fresh_pairs, lengths, residual,
                norm_gain.reshape(1, width), output_weight, expert_gate_up, expert_down,
                routed_experts.T, router_weights.T)
    dma = pltpu.SemaphoreType.DMA
    held = [
        pltpu.SMEM(x.shape, x.dtype) if x is lengths else pltpu.VMEM(x.shape, x.dtype)
        for x in operands
    ]
    return pl.pallas_call(
        functools.partial(layer, sizes),
        out_shape=pltpu.VMEM((rows, share), BF),
        in_specs=[pl.BlockSpec(memory_space=pl.ANY)] * len(operands),
        out_specs=pl.BlockSpec(memory_space=pltpu.VMEM),
        scratch_shapes=held
        + [
            pltpu.VMEM((local_heads, deep, up_to(rows, 16), queries.shape[1] // local_heads), BF),
            pltpu.VMEM((deep, 2 * rows, part // 2), BF),
            pltpu.VMEM((narrow * deep, 2 * rows, part // 2), BF),
            pltpu.VMEM((rows, width), F32),
            pltpu.VMEM((experts, 2 * slots, width // 2), BF),
            pltpu.VMEM((experts, 2 * slots, width // 2), BF),
            pltpu.VMEM((narrow, experts * slots, units), BF),
            pltpu.VMEM((experts, 2 * slots, share // 2), BF),
            pltpu.VMEM((experts, 2 * slots, share // 2), BF),
            dma((len(operands),)),
            dma((local_heads, deep)),
            dma((local_heads, deep)),
            dma((narrow * deep,)),
            dma((narrow * deep,)),
            dma((experts,)),
            dma((experts,)),
            dma((narrow,)),
            dma((narrow,)),
            dma((experts,)),
            dma((experts,)),
        ],
        compiler_params=pltpu.CompilerParams(
            collective_id=0, has_side_effects=True, vmem_limit_bytes=63 * 1024 * 1024
        ),
    )(*operands)


def solution(mesh):
    in_specs = (
        P(("group", "wide", "deep"), "narrow"),
        P(("group", "wide", "deep"), "narrow", None, None),
        P(("group", "wide", "deep"), "narrow", None, None),
        P(("group", "wide", "deep"), None, "narrow"),
        P(("group", "wide", "deep")),
        P(("group", "wide", "deep"), None),
        P(),
        P("narrow", "deep"),
        P(("wide", "deep"), None, "narrow", None),
        P(("wide", "deep"), None, "narrow"),
        P(("group", "wide", "deep"), None),
        P(("group", "wide", "deep"), None),
    )
    out_specs = P(("group", "wide", "deep"), "narrow")
    sizes = (mesh.shape["wide"], mesh.shape["narrow"], mesh.shape["deep"])
    return jax.shard_map(
        functools.partial(shards, sizes), mesh=mesh, in_specs=in_specs, out_specs=out_specs,
        check_vma=False,
    )
```
